256 devices in a mesh: store: 16 (over y, x), batch: 8 (over z), space: 2 (over core).
Axes of the slice: x: 4, y: 4, z: 8, core: 2. Of those that a mesh axis runs over, the one named last changes fastest.
Arguments:
- features: bfloat16 [512, 256, 1024], P(('store', 'batch'), 'space'), may hold values from -24 to 24
- store_maps: bfloat16 [64, 256, 1024], P('store', 'space'), may hold values from -17 to 17
- neighbour_owner: int32 [512, 2], P(('store', 'batch')), may hold values from 0 to 15, all different within a row; in each aligned block of 4 rows (0 to 3, 4 to 7, ...) at most 2 rows name the same one
- neighbour_slot: int32 [512, 2], P(('store', 'batch')), may hold values from 0 to 3
- query_weight: bfloat16 [1024, 1024], P('store', 'space'), may hold values from -0.1875 to 0.1875
- key_weight: bfloat16 [1024, 1024], P('store', 'space'), may hold values from -0.1875 to 0.1875
- value_weight: bfloat16 [1024, 1024], P('store', 'space'), may hold values from -0.1875 to 0.1875
- grad_context: bfloat16 [512, 256, 1024], P(('store', 'batch'), 'space'), may hold values from -6 to 6
Outputs:
- grad_features: bfloat16 [512, 256, 1024], P(('store', 'batch'), 'space')
- grad_query: float32 [1024, 1024], P('store', 'space')
- grad_key: float32 [1024, 1024], P('store', 'space')
- grad_value: float32 [1024, 1024], P('store', 'space')
The draws below stay inside these ranges and needn't reach their ends.
Inputs may be any that keep to these rules, and one draw needn't show every extreme that they name: `neighbour_owner`: within the 4 prompts of one store and batch index, each owner is listed by at most 2 prompts; a prompt's two neighbours have different owners.
All inputs are finite; a program needn't handle non-finite values.
Results may differ from the reference program's by a relative error of at most 0.017.
The reference program's roundings to bfloat16 on the way (of `neighbours`, `weights`, `grad_values` and `dscores`) count: a program that leaves them out, or rounds other values in their place, can miss the bound.
Values may be sent and summed in bfloat16 or wider, within the bound.
No kernel may reach another device: no remote copies, remote signals or barrier semaphores. Data moves between devices by JAX's collectives and lax.ppermute only.
A program may use at most 128 MiB of HBM per device.

```python
import math
import jax
import jax.numpy as jnp
import numpy as np
from jax import lax

C = 1024
INNER = 1024
HD = 64
TOK = 256
P_DEV = 4
MOST = 2
E_DEV = 4
PROMPTS = 512
ENTRIES = 64
N_STORE = 16
N_SPACE = 2


def draw_store_maps(key, part):
    key = jax.random.fold_in(key, 7)
    values = jax.random.normal(key, (ENTRIES, TOK, C), jnp.float32)
    return jnp.clip(values, -8.0, 8.0).astype(jnp.bfloat16)


def set_ends(result, own_key, least, largest):
    longest = result.shape.index(max(result.shape))
    spots = []
    for shift in (0, 1):
        where = [jax.random.randint(jax.random.fold_in(own_key, axis), (), 0, length) for axis, length in enumerate(result.shape)]
        where[longest] = (where[longest] + shift) % result.shape[longest]
        spots.append(tuple(where))
    return result.at[spots[0]].set(least).at[spots[1]].set(largest)


def spiked(array, own_key, source, target, shards_of, factor):
    def block_of(dim):
        return (jnp.arange(array.shape[dim]) // (array.shape[dim] // shards_of)).reshape((-1,) + (1,) * (array.ndim - 1 - dim))

    one_side = jax.random.permutation(own_key, shards_of)[block_of(target)]
    other_side = (block_of(target) + shards_of // 2) % shards_of
    return jnp.where((block_of(source) == one_side) | (block_of(source) == other_side), factor * array, array)


def steps_of(key, dims, pieces, low, largest):
    factor_of = 1.0
    for dim, shards_of in pieces:
        heights = jax.random.uniform(jax.random.fold_in(jax.random.fold_in(key, 6), dim), (shards_of,), jnp.float32, low / len(pieces), largest / len(pieces))
        factor_of = factor_of * jnp.repeat(jnp.exp(heights), dims[dim] // shards_of).reshape((-1,) + (1,) * (len(dims) - 1 - dim))
    return factor_of


def shared_out(own_key, own, number, rows, amount, top, reach, skew):
    order = jax.random.permutation(own_key, amount)
    heavy_load, ordinary = shares(amount, rows * top, reach, skew, True), shares(amount, rows * top, reach, skew, False)
    places = jnp.arange(amount)

    def named(lengths, turn):
        used = int((lengths > 0).sum())
        fixed = max(1, used // 4)
        shifted = fixed + (places - fixed + turn * (used - fixed)) % max(1, amount - fixed)
        return jnp.zeros((amount,), jnp.int32).at[order[jnp.where(places < fixed, places, shifted)]].set(jnp.asarray(lengths, jnp.int32))

    lengths = jnp.where(number % 4 == 0, named(heavy_load, number // 4), named(ordinary, number - number // 4 - 1))
    mixed = jax.random.permutation(jax.random.fold_in(own, 3), amount)
    giver, receiver = mixed[0:amount // 2 * 2:2], mixed[1:amount // 2 * 2:2]
    margin = jnp.minimum(lengths[giver] - 1, reach - lengths[receiver]) // 2
    margin = jnp.where((giver == order[0]) | (receiver == order[0]) | (lengths[receiver] == 0), 0, jnp.maximum(margin, 0))
    shifted = jax.random.randint(jax.random.fold_in(own, 4), (amount // 2,), 0, 1 << 20) % (margin + 1)
    lengths = lengths.at[giver].add(-shifted).at[receiver].add(shifted)
    labels = jnp.searchsorted(jnp.cumsum(lengths), jnp.arange(rows * top), side="right").astype(jnp.int32)
    listing = labels.reshape(top, rows).T
    listing = listing[jax.random.permutation(jax.random.fold_in(own, 1), rows)]
    turn = jax.random.randint(jax.random.fold_in(own, 2), (rows, 1), 0, top)
    return jnp.take_along_axis(listing, (jnp.arange(top)[None, :] + turn) % top, axis=1)


def shares(count, total, reach, slope, full):
    loads = [(1 << 20) // math.isqrt(grade ** slope) + 1 for grade in range(1, count + 1)]
    largest = reach if full else min(reach, max(-(-total // count), total * loads[0] // sum(loads)))
    least = 1 if total - largest >= count - 1 else 0
    given, surplus = [largest] + [least] * (count - 1), total - largest - least * (count - 1)
    while surplus > 0:
        movable = [i for i in range(1, count) if given[i] < largest] or [i for i in range(1, count) if given[i] < reach]
        pool, remaining = sum([loads[i] for i in movable]), surplus
        for i in movable:
            more = min(reach - given[i], max(1, remaining * loads[i] // pool), surplus)
            given[i] = given[i] + more
            surplus = surplus - more
    return np.array(given)


def gaussian(stream_key, shape, deviation, most, cuts=(), dtype=jnp.bfloat16):
    level = steps_of(stream_key, shape, cuts, -0.22, 0.18) if cuts else 1.0
    array = jax.random.normal(stream_key, shape, jnp.float32) * deviation * level
    return jnp.minimum(jnp.maximum(array, -most), most).astype(dtype)


def noise_with(own_key, extent, scale, limit, shards, heavy, held_as=jnp.bfloat16):
    values = scale * jax.random.normal(own_key, extent, jnp.float32)
    if shards:
        values = values * steps_of(own_key, extent, shards, -0.22, 0.18)
    return jnp.clip(spiked(values, jax.random.fold_in(own_key, 3), *heavy), -limit, limit).astype(held_as)


def setup_inputs(seed: int = 0) -> dict:
    key_list = jax.random.split(jax.random.key(seed), 9)
    features = noise_with(key_list[0], (PROMPTS, TOK, C), 1.0, 24.0, ((0, 128), (1, 2)), (0, 2, 128, 5.5))
    store_maps = draw_store_maps(jax.random.fold_in(key_list[8], 71), 0)
    neighbour_owner_keys = jax.random.split(jax.random.fold_in(key_list[2], 1), PROMPTS // P_DEV)
    neighbour_owner_turns = jax.random.permutation(jax.random.fold_in(key_list[2], 3), PROMPTS // P_DEV)
    neighbour_owner = jax.vmap(lambda own, number: shared_out(jax.random.fold_in(key_list[2], 2), own, number, P_DEV, N_STORE, 2, MOST, 2))(neighbour_owner_keys, neighbour_owner_turns).reshape((PROMPTS, 2))
    neighbour_slot = set_ends(jax.random.randint(key_list[3], (PROMPTS, 2), 0, E_DEV), jax.random.fold_in(key_list[3], 1), 0, E_DEV - 1).astype(jnp.int32)
    query_weight = gaussian(key_list[4], (C, INNER), C ** -0.5, 0.1875, ((0, 16), (1, 2)))
    key_weight = gaussian(key_list[5], (C, INNER), C ** -0.5, 0.1875, ((0, 16), (1, 2)))
    value_weight = gaussian(key_list[6], (C, INNER), C ** -0.5, 0.1875, ((0, 16), (1, 2)))
    grad_context = gaussian(key_list[7], (PROMPTS, TOK, INNER), 1.0, 6.0, ((0, 128), (1, 2)))
    return dict(features=features, store_maps=store_maps, neighbour_owner=neighbour_owner, neighbour_slot=neighbour_slot, query_weight=query_weight, key_weight=key_weight, value_weight=value_weight, grad_context=grad_context)


def reference(features, store_maps, neighbour_owner, neighbour_slot, query_weight, key_weight, value_weight, grad_context):
    score_scale = HD ** -0.5
    head_count = INNER // HD
    column_group = INNER // N_SPACE
    index_table = (neighbour_owner * E_DEV + neighbour_slot).astype(jnp.int32)

    def prompt_step(carry, inputs):
        grad_q_sum, grad_k_sum, grad_v_sum = carry
        prompt_rows, picked, upstream_rows = inputs
        neighbours = jnp.take(store_maps, picked, axis=0).reshape(2 * TOK, C)
        query = jnp.dot(prompt_rows, query_weight, preferred_element_type=jnp.float32).astype(jnp.bfloat16)
        keys = jnp.dot(neighbours, key_weight, preferred_element_type=jnp.float32).astype(jnp.bfloat16)
        values = jnp.dot(neighbours, value_weight, preferred_element_type=jnp.float32).astype(jnp.bfloat16)
        query_heads = query.reshape(TOK, head_count, HD).astype(jnp.float32)
        key_heads = keys.reshape(2 * TOK, head_count, HD).astype(jnp.float32)
        value_heads = values.reshape(2 * TOK, head_count, HD).astype(jnp.float32)
        scores = jnp.einsum("thd,shd->hts", query_heads, key_heads) * score_scale
        attention = jax.nn.softmax(scores, axis=-1)
        weights = attention.astype(jnp.bfloat16)
        weights_wide = weights.astype(jnp.float32)
        upstream = upstream_rows.reshape(TOK, head_count, HD).astype(jnp.float32)
        dweights = jnp.einsum("thd,shd->hts", upstream, value_heads)
        grad_values = jnp.einsum("hts,thd->shd", weights_wide, upstream).astype(jnp.bfloat16)
        dscores = (attention * (dweights - jnp.sum(attention * dweights, axis=-1, keepdims=True))).astype(jnp.bfloat16)
        dscores_wide = dscores.astype(jnp.float32)
        grad_query_rows = (jnp.einsum("hts,shd->thd", dscores_wide, key_heads) * score_scale).astype(jnp.bfloat16)
        grad_keys = (jnp.einsum("hts,thd->shd", dscores_wide, query_heads) * score_scale).astype(jnp.bfloat16)
        grad_query_rows = grad_query_rows.reshape(TOK, INNER)
        grad_keys = grad_keys.reshape(2 * TOK, INNER)
        grad_values = grad_values.reshape(2 * TOK, INNER)
        total_rows = jnp.zeros((TOK, C), jnp.float32)
        for group in range(N_SPACE):
            first = group * column_group
            partial_rows = jnp.dot(grad_query_rows[:, first:first + column_group], query_weight[:, first:first + column_group].T, preferred_element_type=jnp.float32).astype(jnp.bfloat16)
            partial_rows = lax.optimization_barrier(partial_rows)
            total_rows = total_rows + partial_rows.astype(jnp.float32)
        grad_rows = total_rows.astype(jnp.bfloat16)
        contract = (((0,), (0,)), ((), ()))
        grad_q_sum = grad_q_sum + lax.dot_general(prompt_rows, grad_query_rows, contract, preferred_element_type=jnp.float32)
        grad_k_sum = grad_k_sum + lax.dot_general(neighbours, grad_keys, contract, preferred_element_type=jnp.float32)
        grad_v_sum = grad_v_sum + lax.dot_general(neighbours, grad_values, contract, preferred_element_type=jnp.float32)
        return (grad_q_sum, grad_k_sum, grad_v_sum), grad_rows

    zeros = jnp.zeros((C, INNER), jnp.float32)
    sums, grad_features = lax.scan(prompt_step, (zeros, zeros, zeros), (features, index_table, grad_context))
    return (grad_features, sums[0], sums[1], sums[2])
```

```python
import functools

import jax
import jax.numpy as jnp
from jax import lax
from jax.experimental import pallas as pl
from jax.experimental.pallas import tpu as pltpu
from jax.sharding import PartitionSpec as P

HD = 64
F32 = jnp.float32
BF16 = jnp.bfloat16
NT = (((1,), (1,)), ((), ()))
TN = (((0,), (0,)), ((), ()))


def pick_kernel(where_ref, table_ref, *outs):
    layers, per = outs[0].shape[:2]
    for number, out in enumerate(outs):
        for layer in range(layers):
            for item in range(per):
                place = where_ref[(number * layers + layer) * per + item]
                out[layer, item] = table_ref[place]


def pick(table, where, chunks, layers, per):
    rows, channels = table.shape[1:]
    vmem = pl.BlockSpec(memory_space=pltpu.VMEM)
    return pl.pallas_call(
        pick_kernel,
        out_shape=[jax.ShapeDtypeStruct((layers, per, rows, channels), table.dtype)] * chunks,
        in_specs=[pl.BlockSpec(memory_space=pltpu.SMEM), vmem],
        out_specs=[vmem] * chunks,
        compiler_params=pltpu.CompilerParams(vmem_limit_bytes=16 * 2**20),
        name="pick",
    )(where, table)


def attention_kernel(
    xo, xt, uo, ut, no, nt, wq, wk, wv, gq, gk, gv, q_s, k_s, v_s, u_s
):
    half = xo.shape[1]
    tokens = 2 * half
    layers, _, rows, channels = no.shape
    part = layers * rows
    own, other = no[...].reshape(part, channels), nt[...].reshape(part, channels)
    q_s[:half] = jnp.dot(xo[0], wq[...], preferred_element_type=F32).astype(BF16)
    q_s[half:] = jnp.dot(xt[0], wq[...], preferred_element_type=F32).astype(BF16)
    k_s[:part] = jnp.dot(own, wk[...], preferred_element_type=F32).astype(BF16)
    k_s[part:] = jnp.dot(other, wk[...], preferred_element_type=F32).astype(BF16)
    v_s[:part] = jnp.dot(own, wv[...], preferred_element_type=F32).astype(BF16)
    v_s[part:] = jnp.dot(other, wv[...], preferred_element_type=F32).astype(BF16)
    u_s[:half] = uo[0]
    u_s[half:] = ut[0]
    width = q_s.shape[1]
    scale = HD ** (-0.5)
    lane = lax.broadcasted_iota(jnp.int32, (1, 2 * HD), 1)
    first = lane < HD
    for pair in range(width // (2 * HD)):
        cols = pl.ds(pair * 2 * HD, 2 * HD)
        kp, vp = k_s[:, cols], v_s[:, cols]
        grad_k = grad_v = None
        grad_q = []
        for side in range(2):
            keep = jnp.where(first if side == 0 else jnp.logical_not(first), 1.0, 0.0)
            qm = q_s[:, cols] * (keep * scale).astype(BF16)
            um = u_s[:, cols] * keep.astype(BF16)
            s = lax.dot_general(kp, qm, NT, preferred_element_type=F32)
            e = jnp.exp(s - jnp.max(s, axis=0, keepdims=True))
            att = e * (1.0 / jnp.sum(e, axis=0, keepdims=True))
            dw = lax.dot_general(vp, um, NT, preferred_element_type=F32)
            gv_part = jnp.dot(att.astype(BF16), um, preferred_element_type=F32)
            row = jnp.sum(att * dw, axis=0, keepdims=True)
            ds = (att * (dw - row)).astype(BF16)
            gk_part = jnp.dot(ds, qm, preferred_element_type=F32)
            grad_q.append(lax.dot_general(ds, kp, TN, preferred_element_type=F32))
            grad_v = gv_part if grad_v is None else grad_v + gv_part
            grad_k = gk_part if grad_k is None else grad_k + gk_part
        gq[0, :, cols] = (jnp.where(first, grad_q[0], grad_q[1]) * scale).astype(BF16)
        gk[0, :, cols] = grad_k.astype(BF16)
        gv[0, :, cols] = grad_v.astype(BF16)


def attention(xo, xt, uo, ut, no, nt, weights, first_prompt):
    layers, prompts, rows, channels = no.shape
    part = layers * rows
    half = xo.shape[1]
    local = weights.shape[1] // 3
    step = min(local, 4 * HD)
    steps = local // step
    token_spec = pl.BlockSpec((1, half, channels), lambda p, c: (p + first_prompt, 0, 0))
    up_spec = pl.BlockSpec((1, half, step), lambda p, c: (p + first_prompt, 0, c))
    map_spec = pl.BlockSpec((layers, 1, rows, channels), lambda p, c: (0, p, 0, 0))
    w_specs = [
        pl.BlockSpec((channels, step), lambda p, c, i=i: (0, c + i * steps)) for i in range(3)
    ]
    flops = prompts * 2 * (2 * half * channels * local + 4 * part * channels * local) + (
        prompts * 2 * local * 5 * 2 * half * 2 * part
    )
    return pl.pallas_call(
        attention_kernel,
        grid=(prompts, steps),
        out_shape=[
            jax.ShapeDtypeStruct((prompts, 2 * half, local), BF16),
            jax.ShapeDtypeStruct((prompts, 2 * part, local), BF16),
            jax.ShapeDtypeStruct((prompts, 2 * part, local), BF16),
        ],
        in_specs=[token_spec, token_spec, up_spec, up_spec, map_spec, map_spec] + w_specs,
        out_specs=[
            pl.BlockSpec((1, 2 * half, step), lambda p, c: (p, 0, c)),
            pl.BlockSpec((1, 2 * part, step), lambda p, c: (p, 0, c)),
            pl.BlockSpec((1, 2 * part, step), lambda p, c: (p, 0, c)),
        ],
        scratch_shapes=[
            pltpu.VMEM((2 * half, step), BF16),
            pltpu.VMEM((2 * part, step), BF16),
            pltpu.VMEM((2 * part, step), BF16),
            pltpu.VMEM((2 * half, step), BF16),
        ],
        compiler_params=pltpu.CompilerParams(vmem_limit_bytes=40 * 2**20),
        cost_estimate=pl.CostEstimate(
            flops=2 * flops, bytes_accessed=12 * 2**20, transcendentals=prompts * 2**20
        ),
        name="attention",
    )(xo, xt, uo, ut, no, nt, weights, weights, weights)


def hold(array, after):
    anywhere = pl.BlockSpec(memory_space=pl.ANY)
    return pl.pallas_call(
        lambda array_ref, after_ref, out_ref: None,
        out_shape=jax.ShapeDtypeStruct(array.shape, array.dtype),
        in_specs=[anywhere, anywhere],
        out_specs=anywhere,
        input_output_aliases={0: 0},
        name="hold",
    )(array, after)


def weights_kernel(first_prompt, keep, *refs):
    xo, xt, no, nt, gq, gk, gv = refs[:7]
    before, out = (None, refs[7]) if keep else (refs[7], refs[8])
    prompts = gq.shape[0]
    layers, _, rows, width = no.shape
    local = gq.shape[2]
    tokens, maps = [], []
    for p in range(prompts):
        tokens += [xo[first_prompt + p], xt[first_prompt + p]]
        maps += [no[:, p].reshape(layers * rows, width), nt[:, p].reshape(layers * rows, width)]
    tokens, maps = jnp.concatenate(tokens, axis=0), jnp.concatenate(maps, axis=0)
    for i, (left, grad) in enumerate(((tokens, gq), (maps, gk), (maps, gv))):
        cols = pl.ds(i * local, local)
        total = lax.dot_general(
            left, grad[...].reshape(-1, local), TN, preferred_element_type=F32
        )
        if before is not None:
            total = total + before[:, cols]
        out[:, cols] = total.astype(out.dtype)


def weight_grads(xo, xt, no, nt, gq, gk, gv, before, first_prompt):
    prompts, half, channels = xo.shape
    layers, per_chunk, rows, _ = no.shape
    local = gq.shape[2]
    width = 256
    keep = before is None
    token_spec = pl.BlockSpec((prompts, half, width), lambda c: (0, 0, c))
    map_spec = pl.BlockSpec((layers, per_chunk, rows, width), lambda c: (0, 0, 0, c))
    grad_specs = [pl.BlockSpec(g.shape, lambda c: (0, 0, 0)) for g in (gq, gk, gv)]
    out_spec = pl.BlockSpec((width, 3 * local), lambda c: (c, 0))
    extra = [] if keep else [before]
    return pl.pallas_call(
        functools.partial(weights_kernel, first_prompt, keep),
        grid=(channels // width,),
        out_shape=jax.ShapeDtypeStruct((channels, 3 * local), F32 if keep else BF16),
        in_specs=[token_spec, token_spec, map_spec, map_spec]
        + grad_specs
        + [out_spec] * len(extra),
        out_specs=out_spec,
        compiler_params=pltpu.CompilerParams(vmem_limit_bytes=40 * 2**20),
        cost_estimate=pl.CostEstimate(
            flops=2 * channels * local * per_chunk * (2 * half + 4 * layers * rows),
            bytes_accessed=12 * 2**20,
            transcendentals=0,
        ),
        name="weight_grads",
    )(xo, xt, no, nt, gq, gk, gv, *extra)


def per_device(
    features,
    store_maps,
    neighbour_owner,
    neighbour_slot,
    query_weight,
    key_weight,
    value_weight,
    grad_context,
):
    prompts, half, channels = features.shape
    entries = store_maps.shape[0]
    owners = lax.axis_size("store")
    layers = lax.axis_size("batch")
    local = query_weight.shape[1]
    layer, core = lax.axis_index("batch"), lax.axis_index("space")
    swap = [(0, 1), (1, 0)]

    share = half // layers
    mine = lax.dynamic_slice_in_dim(store_maps, layer * share, share, axis=1)
    table = lax.all_to_all(
        jnp.broadcast_to(mine[None], (owners,) + mine.shape),
        "store",
        split_axis=0,
        concat_axis=0,
        tiled=True,
    ).reshape(owners * entries, share, channels)

    listed = (neighbour_owner * entries + neighbour_slot).reshape(1, -1)
    reach = 1
    while reach < layers:
        moved = lax.ppermute(
            listed, "batch", [(z, (z + reach) % layers) for z in range(layers)]
        )
        listed = jnp.concatenate([listed, moved], axis=0)
        reach *= 2
    place = jnp.roll(listed[::-1], layer + 1, axis=0)
    chunks = 2
    per_chunk = prompts // chunks
    per = 2 * per_chunk
    order = place.reshape(layers, chunks, per).transpose(1, 0, 2).reshape(-1)
    picked = pick(table, order, chunks, layers, per)

    packed = jnp.concatenate([query_weight, key_weight, value_weight], axis=1)
    weights = lax.all_gather(packed, "store", axis=0, tiled=True)
    full_query = weights[:, :local]

    x_other = lax.ppermute(features, "space", swap)
    u_own = lax.dynamic_slice_in_dim(grad_context, core * local, local, axis=2)
    u_send = lax.dynamic_slice_in_dim(grad_context, (1 - core) * local, local, axis=2)
    u_other = lax.ppermute(u_send, "space", swap)

    sums = gq = None
    features_out = []
    for chunk in range(chunks):
        n_own = lax.all_to_all(
            picked[chunk], "batch", split_axis=0, concat_axis=0, tiled=True
        ).reshape(layers, per_chunk, 2 * share, channels)
        if gq is not None:
            n_own = hold(n_own, gq)
        n_other = lax.ppermute(n_own, "space", swap)
        begin = chunk * per_chunk
        gq, gk, gv = attention(
            features, x_other, u_own, u_other, n_own, n_other, weights, begin
        )
        part = half * 2
        partial_rows = jnp.dot(
            gq.reshape(per_chunk * part, local).reshape(per_chunk, 2, half, local),
            full_query.T,
            preferred_element_type=F32,
        ).astype(BF16)
        received = lax.ppermute(partial_rows[:, 1], "space", swap)
        features_out.append(
            (partial_rows[:, 0].astype(F32) + received.astype(F32)).astype(BF16)
        )

        sums = weight_grads(features, x_other, n_own, n_other, gq, gk, gv, sums, begin)
    grad_features = jnp.concatenate(features_out, axis=0)

    row_share = channels // owners
    sent = sums.reshape(owners, row_share, 3 * local)
    came = lax.all_to_all(sent, "store", split_axis=0, concat_axis=0, tiled=True)
    layer_sum = jnp.sum(came.astype(F32), axis=0)
    pieces = layer_sum.reshape(layers, row_share // layers, 3 * local)
    crossed = lax.all_to_all(pieces, "batch", split_axis=0, concat_axis=0, tiled=True)
    summed = jnp.sum(crossed, axis=0, keepdims=True)
    totals = lax.all_to_all(
        jnp.broadcast_to(summed, pieces.shape), "batch", split_axis=0, concat_axis=0, tiled=True
    ).reshape(row_share, 3 * local)
    return (
        grad_features,
        totals[:, :local],
        totals[:, local : 2 * local],
        totals[:, 2 * local :],
    )


def solution(mesh):
    in_specs = (
        P(("store", "batch"), "space", None),
        P("store", "space", None),
        P(("store", "batch"), None),
        P(("store", "batch"), None),
        P("store", "space"),
        P("store", "space"),
        P("store", "space"),
        P(("store", "batch"), "space", None),
    )
    out_specs = (
        P(("store", "batch"), "space", None),
        P("store", "space"),
        P("store", "space"),
        P("store", "space"),
    )
    return jax.shard_map(
        per_device, mesh=mesh, in_specs=in_specs, out_specs=out_specs, check_vma=False
    )
```

```python
import functools

import jax
import jax.numpy as jnp
from jax import lax
from jax.experimental import pallas as pl
from jax.experimental.pallas import tpu as pltpu
from jax.sharding import PartitionSpec as P

HD = 64
VMEM_BYTES = 60 * 2**20
F32 = jnp.float32
BF16 = jnp.bfloat16
NT = (((1,), (1,)), ((), ()))
TN = (((0,), (0,)), ((), ()))


def prepare_kernel(layer_ref, maps_ref, wq, wk, wv, table_ref, packed_ref):
    owners, _, share, _ = table_ref.shape
    begin = pl.multiple_of(layer_ref[0] * share, share)
    mine = maps_ref[:, pl.ds(begin, share), :]
    for owner in range(owners):
        table_ref[owner] = mine
    local = wq.shape[1]
    for i, w in enumerate((wq, wk, wv)):
        packed_ref[:, pl.ds(i * local, local)] = w[...]


def prepare(layer, store_maps, wq, wk, wv, owners, share):
    entries, _, channels = store_maps.shape
    rows, local = wq.shape
    vmem = pl.BlockSpec(memory_space=pltpu.VMEM)
    return pl.pallas_call(
        prepare_kernel,
        out_shape=[
            jax.ShapeDtypeStruct((owners, entries, share, channels), BF16),
            jax.ShapeDtypeStruct((rows, 3 * local), BF16),
        ],
        in_specs=[pl.BlockSpec(memory_space=pltpu.SMEM)] + [vmem] * 4,
        out_specs=[vmem] * 2,
        compiler_params=pltpu.CompilerParams(vmem_limit_bytes=16 * 2**20),
        name="prepare",
    )(layer.reshape(1).astype(jnp.int32), store_maps, wq, wk, wv)


def pick_kernel(where_ref, table_ref, *outs):
    layers, per = outs[0].shape[:2]
    for number, out in enumerate(outs):
        for layer in range(layers):
            for item in range(per):
                place = where_ref[(number * layers + layer) * per + item]
                out[layer, item] = table_ref[place]


def pick(table, where, chunks, layers, per):
    rows, channels = table.shape[1:]
    vmem = pl.BlockSpec(memory_space=pltpu.VMEM)
    return pl.pallas_call(
        pick_kernel,
        out_shape=[jax.ShapeDtypeStruct((layers, per, rows, channels), table.dtype)] * chunks,
        in_specs=[pl.BlockSpec(memory_space=pltpu.SMEM), vmem],
        out_specs=[vmem] * chunks,
        compiler_params=pltpu.CompilerParams(vmem_limit_bytes=16 * 2**20),
        name="pick",
    )(where, table)


def attention_kernel(has_before, *refs):
    xo, xt, uo, ut, no, nt, wq, wk, wv = refs[:9]
    before = refs[9] if has_before else None
    gqo, gqt, sums, q_s, k_s, v_s, gq_s, gkv_s = refs[9 + has_before :]
    prompts, half, channels = xo.shape
    layers, _, rows, _ = no.shape
    part = layers * rows
    width = wq.shape[1]
    tokens, maps = (xo, xt), (no, nt)
    for i in range(2):
        x = tokens[i][...].reshape(prompts * half, channels)
        n = maps[i][...].reshape(prompts * part, channels)
        q = jnp.dot(x, wq[...], preferred_element_type=F32).astype(BF16)
        k = jnp.dot(n, wk[...], preferred_element_type=F32).astype(BF16)
        v = jnp.dot(n, wv[...], preferred_element_type=F32).astype(BF16)
        q_s[i] = q.reshape(prompts, half, width)
        k_s[i] = k.reshape(layers, prompts, rows, width)
        v_s[i] = v.reshape(layers, prompts, rows, width)
    scale = HD ** (-0.5)
    lane = lax.broadcasted_iota(jnp.int32, (1, 2 * HD), 1)
    first = lane < HD

    def both(array):
        return jnp.concatenate([array[0], array[1]], axis=0)

    for p in range(prompts):
        for pair in range(width // (2 * HD)):
            cols = pl.ds(pair * 2 * HD, 2 * HD)
            kp = both([k_s[i, :, p, :, cols].reshape(part, 2 * HD) for i in range(2)])
            vp = both([v_s[i, :, p, :, cols].reshape(part, 2 * HD) for i in range(2)])
            qp = both([q_s[i, p, :, cols] for i in range(2)])
            up = both([uo[p, :, cols], ut[p, :, cols]])
            kt = kp.T
            grad_k = grad_v = None
            grad_q = []
            for side in range(2):
                keep = jnp.where(first if side == 0 else jnp.logical_not(first), 1.0, 0.0)
                qm = qp * (keep * scale).astype(BF16)
                um = up * keep.astype(BF16)
                s = lax.dot_general(kp, qm, NT, preferred_element_type=F32)
                dw = lax.dot_general(vp, um, NT, preferred_element_type=F32)
                e = jnp.exp(s - jnp.max(s, axis=0, keepdims=True))
                inverse = 1.0 / jnp.sum(e, axis=0, keepdims=True)
                att = e * inverse
                row = jnp.sum(e * dw, axis=0, keepdims=True) * inverse
                gv_part = jnp.dot(att.astype(BF16), um, preferred_element_type=F32)
                ds = (att * (dw - row)).astype(BF16)
                gk_part = jnp.dot(ds, qm, preferred_element_type=F32)
                grad_q.append(
                    jnp.dot(kt[side * HD : (side + 1) * HD], ds, preferred_element_type=F32)
                )
                grad_v = gv_part if grad_v is None else grad_v + gv_part
                grad_k = gk_part if grad_k is None else grad_k + gk_part
            gq = (both(grad_q) * scale).T.astype(BF16)
            gk, gv = grad_k.astype(BF16), grad_v.astype(BF16)
            more = pl.ds(width + pair * 2 * HD, 2 * HD)
            for i, out in enumerate((gqo, gqt)):
                out[p, :, cols] = gq[i * half : (i + 1) * half]
                gq_s[i, p, :, cols] = gq[i * half : (i + 1) * half]
                here = slice(i * part, (i + 1) * part)
                gkv_s[i, :, p, :, cols] = gk[here].reshape(layers, rows, 2 * HD)
                gkv_s[i, :, p, :, more] = gv[here].reshape(layers, rows, 2 * HD)
    gq_all = gq_s[...].reshape(2 * prompts * half, width)
    gkv_all = gkv_s[...].reshape(2 * prompts * part, 2 * width)
    block = 256
    for begin in range(0, channels, block):
        at = pl.ds(begin, block)
        x = both([t[:, :, at].reshape(prompts * half, block) for t in tokens])
        n = both([t[:, :, :, at].reshape(prompts * part, block) for t in maps])
        dq = lax.dot_general(x, gq_all, TN, preferred_element_type=F32)
        dkv = lax.dot_general(n, gkv_all, TN, preferred_element_type=F32)
        for i, total in enumerate((dq, dkv[:, :width], dkv[:, width:])):
            if before is None:
                sums[i, at] = total
            else:
                total = (total + before[i, at]).astype(BF16)
                share = sums.shape[2]
                own = begin // share
                sums[own : own + block // share, i] = total.reshape(
                    block // share, share, width
                )


def attention(xo, xt, uo, ut, no, nt, weights, before, chunk, owners):
    layers, prompts, rows, channels = no.shape
    half = xo.shape[1]
    part = layers * rows
    local = weights.shape[1] // 3
    step = min(local, 4 * HD)
    steps = local // step
    token_spec = pl.BlockSpec((prompts, half, channels), lambda c: (chunk, 0, 0))
    up_spec = pl.BlockSpec((prompts, half, step), lambda c: (chunk, 0, c))
    map_spec = pl.BlockSpec(no.shape, lambda c: (0, 0, 0, 0))
    w_specs = [
        pl.BlockSpec((channels, step), lambda c, i=i: (0, c + i * steps)) for i in range(3)
    ]
    grad_spec = pl.BlockSpec((prompts, half, step), lambda c: (0, 0, c))
    wide_spec = pl.BlockSpec((3, channels, step), lambda c: (0, 0, c))
    has_before = before is not None
    if has_before:
        share = channels // owners
        sum_shape = jax.ShapeDtypeStruct((owners, 3, share, local), BF16)
        sum_spec = pl.BlockSpec((owners, 3, share, step), lambda c: (0, 0, 0, c))
    else:
        sum_shape = jax.ShapeDtypeStruct((3, channels, local), F32)
        sum_spec = wide_spec
    return pl.pallas_call(
        functools.partial(attention_kernel, has_before),
        grid=(steps,),
        out_shape=[jax.ShapeDtypeStruct((prompts, half, local), BF16)] * 2 + [sum_shape],
        in_specs=[token_spec, token_spec, up_spec, up_spec, map_spec, map_spec]
        + w_specs
        + [wide_spec] * has_before,
        out_specs=[grad_spec, grad_spec, sum_spec],
        scratch_shapes=[
            pltpu.VMEM((2, prompts, half, step), BF16),
            pltpu.VMEM((2, layers, prompts, rows, step), BF16),
            pltpu.VMEM((2, layers, prompts, rows, step), BF16),
            pltpu.VMEM((2, prompts, half, step), BF16),
            pltpu.VMEM((2, layers, prompts, rows, 2 * step), BF16),
        ],
        compiler_params=pltpu.CompilerParams(vmem_limit_bytes=VMEM_BYTES),
        cost_estimate=pl.CostEstimate(
            flops=prompts * 2 * 2 * (2 * half + 4 * part) * channels * local,
            bytes_accessed=16 * 2**20,
            transcendentals=prompts * 2 * half * 2 * part * (local // HD),
        ),
        name="attention",
    )(xo, xt, uo, ut, no, nt, weights, weights, weights, *([before] if has_before else []))


def hold(array, after):
    anywhere = pl.BlockSpec(memory_space=pl.ANY)
    return pl.pallas_call(
        lambda array_ref, after_ref, out_ref: None,
        out_shape=jax.ShapeDtypeStruct(array.shape, array.dtype),
        in_specs=[anywhere, anywhere],
        out_specs=anywhere,
        input_output_aliases={0: 0},
        name="hold",
    )(array, after)


def per_device(
    features,
    store_maps,
    neighbour_owner,
    neighbour_slot,
    query_weight,
    key_weight,
    value_weight,
    grad_context,
):
    prompts, half, channels = features.shape
    entries = store_maps.shape[0]
    owners = lax.axis_size("store")
    layers = lax.axis_size("batch")
    local = query_weight.shape[1]
    layer, core = lax.axis_index("batch"), lax.axis_index("space")
    swap = [(0, 1), (1, 0)]

    share = half // layers
    spread, packed = prepare(
        layer, store_maps, query_weight, key_weight, value_weight, owners, share
    )
    table = lax.all_to_all(
        spread, "store", split_axis=0, concat_axis=0, tiled=True
    ).reshape(owners * entries, share, channels)

    listed = (neighbour_owner * entries + neighbour_slot).reshape(1, -1)
    reach = 1
    while reach < layers:
        moved = lax.ppermute(
            listed, "batch", [(z, (z + reach) % layers) for z in range(layers)]
        )
        listed = jnp.concatenate([listed, moved], axis=0)
        reach *= 2
    place = jnp.roll(listed[::-1], layer + 1, axis=0)
    chunks = 2
    per_chunk = prompts // chunks
    per = 2 * per_chunk
    order = place.reshape(layers, chunks, per).transpose(1, 0, 2).reshape(-1)
    picked = pick(table, order, chunks, layers, per)

    weights = lax.all_gather(packed, "store", axis=0, tiled=True)
    full_query = weights[:, :local]

    x_other = lax.ppermute(features, "space", swap)
    u_own = lax.dynamic_slice_in_dim(grad_context, core * local, local, axis=2)
    u_send = lax.dynamic_slice_in_dim(grad_context, (1 - core) * local, local, axis=2)
    u_other = lax.ppermute(u_send, "space", swap)

    sums = gq = None
    features_out = []
    for chunk in range(chunks):
        n_own = lax.all_to_all(
            picked[chunk], "batch", split_axis=0, concat_axis=0, tiled=True
        ).reshape(layers, per_chunk, 2 * share, channels)
        if gq is not None:
            n_own = hold(n_own, gq)
        n_other = lax.ppermute(n_own, "space", swap)
        gq, gq_other, sums = attention(
            features, x_other, u_own, u_other, n_own, n_other, weights, sums, chunk, owners
        )

        def rows_of(grad):
            product = lax.dot_general(
                grad, full_query, (((2,), (1,)), ((), ())), preferred_element_type=F32
            )
            return lax.reduce_precision(product, exponent_bits=8, mantissa_bits=7)

        received = lax.ppermute(rows_of(gq_other).astype(BF16), "space", swap)
        features_out.append((rows_of(gq) + received.astype(F32)).astype(BF16))
    grad_features = jnp.concatenate(features_out, axis=0)

    row_share = channels // owners
    came = lax.all_to_all(sums, "store", split_axis=0, concat_axis=0, tiled=True)
    layer_sum = jnp.sum(came.astype(F32), axis=0)
    share = row_share // layers
    pieces = layer_sum.reshape(3, layers, share, local).transpose(1, 0, 2, 3)
    crossed = lax.all_to_all(pieces, "batch", split_axis=0, concat_axis=0, tiled=True)
    summed = jnp.sum(crossed, axis=0, keepdims=True)
    totals = lax.all_to_all(
        jnp.broadcast_to(summed, pieces.shape), "batch", split_axis=0, concat_axis=0, tiled=True
    )
    grads = [totals[:, i].reshape(row_share, local) for i in range(3)]
    return (grad_features, *grads)


def solution(mesh):
    in_specs = (
        P(("store", "batch"), "space", None),
        P("store", "space", None),
        P(("store", "batch"), None),
        P(("store", "batch"), None),
        P("store", "space"),
        P("store", "space"),
        P("store", "space"),
        P(("store", "batch"), "space", None),
    )
    out_specs = (
        P(("store", "batch"), "space", None),
        P("store", "space"),
        P("store", "space"),
        P("store", "space"),
    )
    return jax.shard_map(
        per_device, mesh=mesh, in_specs=in_specs, out_specs=out_specs, check_vma=False
    )
```

```python
import functools

import jax
import jax.numpy as jnp
from jax import lax
from jax.experimental import pallas as pl
from jax.experimental.pallas import tpu as pltpu
from jax.sharding import PartitionSpec as P

HD = 64
VMEM_BYTES = 60 * 2**20
F32 = jnp.float32
BF16 = jnp.bfloat16
NT = (((1,), (1,)), ((), ()))
TN = (((0,), (0,)), ((), ()))


def whole(memory):
    return pl.BlockSpec(memory_space=memory)


def prepare_kernel(layer_ref, maps_ref, wq, wk, wv, table_ref, packed_ref):
    owners, _, share, _ = table_ref.shape
    begin = pl.multiple_of(layer_ref[0] * share, share)
    mine = maps_ref[:, pl.ds(begin, share), :]
    for owner in range(owners):
        table_ref[owner] = mine
    local = wq.shape[1]
    for i, w in enumerate((wq, wk, wv)):
        packed_ref[:, pl.ds(i * local, local)] = w[...]


def prepare(layer, store_maps, wq, wk, wv, owners, share):
    entries, _, channels = store_maps.shape
    rows, local = wq.shape
    vmem = pl.BlockSpec(memory_space=pltpu.VMEM)
    return pl.pallas_call(
        prepare_kernel,
        out_shape=[
            jax.ShapeDtypeStruct((owners, entries, share, channels), BF16),
            jax.ShapeDtypeStruct((rows, 3 * local), BF16),
        ],
        in_specs=[pl.BlockSpec(memory_space=pltpu.SMEM)] + [vmem] * 4,
        out_specs=[vmem] * 2,
        compiler_params=pltpu.CompilerParams(vmem_limit_bytes=VMEM_BYTES),
        name="prepare",
    )(layer.reshape(1).astype(jnp.int32), store_maps, wq, wk, wv)


def total_kernel(parts_ref, out_ref):
    total = parts_ref[0]
    for i in range(1, parts_ref.shape[0]):
        total = total + parts_ref[i]
    for i in range(out_ref.shape[0]):
        out_ref[i] = total


def total_for_all(parts):
    return pl.pallas_call(
        total_kernel,
        out_shape=jax.ShapeDtypeStruct(parts.shape, parts.dtype),
        in_specs=[whole(pltpu.VMEM)],
        out_specs=whole(pltpu.VMEM),
        compiler_params=pltpu.CompilerParams(vmem_limit_bytes=16 * 2**20),
        name="total",
    )(parts)


def pick_kernel(waits, where_ref, table_ref, *refs):
    outs = refs[waits:]
    layers, per = outs[0].shape[:2]
    for number, out in enumerate(outs):
        for layer in range(layers):
            for item in range(per):
                place = where_ref[(number * layers + layer) * per + item]
                out[layer, item] = table_ref[place]


def pick(table, where, chunks, layers, per, after):
    rows, channels = table.shape[1:]
    vmem = pl.BlockSpec(memory_space=pltpu.VMEM)
    return pl.pallas_call(
        functools.partial(pick_kernel, len(after)),
        out_shape=[jax.ShapeDtypeStruct((layers, per, rows, channels), table.dtype)] * chunks,
        in_specs=[whole(pltpu.SMEM), vmem] + [whole(pl.ANY)] * len(after),
        out_specs=[vmem] * chunks,
        compiler_params=pltpu.CompilerParams(vmem_limit_bytes=16 * 2**20),
        name="pick",
    )(where, table, *after)


def attention_kernel(has_before, core_ref, *refs):
    xo, xt, uo, ut, no, nt, wq, wk, wv = refs[:9]
    before = refs[9] if has_before else None
    gqo, gqt, sums, q_s, k_s, v_s, gq_s, gkv_s = refs[9 + has_before :]
    prompts, half, channels = xo.shape
    layers, _, rows, _ = no.shape
    part = layers * rows
    width = wq.shape[1]
    tokens, maps = (xo, xt), (no, nt)
    for i in range(2):
        x = tokens[i][...].reshape(prompts * half, channels)
        n = maps[i][...].reshape(prompts * part, channels)
        q = jnp.dot(x, wq[...], preferred_element_type=F32).astype(BF16)
        k = jnp.dot(n, wk[...], preferred_element_type=F32).astype(BF16)
        v = jnp.dot(n, wv[...], preferred_element_type=F32).astype(BF16)
        q_s[i] = q.reshape(prompts, half, width)
        k_s[i] = k.reshape(layers, prompts, rows, width)
        v_s[i] = v.reshape(layers, prompts, rows, width)
    scale = HD ** (-0.5)
    lane = lax.broadcasted_iota(jnp.int32, (1, 2 * HD), 1)
    first = lane < HD

    def both(array):
        return jnp.concatenate([array[0], array[1]], axis=0)

    for p in range(prompts):
        for pair in range(width // (2 * HD)):
            cols = pl.ds(pair * 2 * HD, 2 * HD)
            kp = both([k_s[i, :, p, :, cols].reshape(part, 2 * HD) for i in range(2)])
            vp = both([v_s[i, :, p, :, cols].reshape(part, 2 * HD) for i in range(2)])
            qp = both([q_s[i, p, :, cols] for i in range(2)])
            up = both([uo[p, :, cols], ut[p, :, cols]])
            kt = kp.T
            grad_k = grad_v = None
            grad_q = []
            for side in range(2):
                keep = jnp.where(first if side == 0 else jnp.logical_not(first), 1.0, 0.0)
                qm = qp * (keep * scale).astype(BF16)
                um = up * keep.astype(BF16)
                s = lax.dot_general(kp, qm, NT, preferred_element_type=F32)
                dw = lax.dot_general(vp, um, NT, preferred_element_type=F32)
                e = jnp.exp(s - jnp.max(s, axis=0, keepdims=True))
                inverse = 1.0 / jnp.sum(e, axis=0, keepdims=True)
                att = e * inverse
                row = jnp.sum(e * dw, axis=0, keepdims=True) * inverse
                gv_part = jnp.dot(att.astype(BF16), um, preferred_element_type=F32)
                ds = (att * (dw - row)).astype(BF16)
                gk_part = jnp.dot(ds, qm, preferred_element_type=F32)
                grad_q.append(
                    jnp.dot(kt[side * HD : (side + 1) * HD], ds, preferred_element_type=F32)
                )
                grad_v = gv_part if grad_v is None else grad_v + gv_part
                grad_k = gk_part if grad_k is None else grad_k + gk_part
            gq = (both(grad_q) * scale).T.astype(BF16)
            gk, gv = grad_k.astype(BF16), grad_v.astype(BF16)
            more = pl.ds(width + pair * 2 * HD, 2 * HD)
            for i, out in enumerate((gqo, gqt)):
                out[p, :, cols] = gq[i * half : (i + 1) * half]
                gq_s[i, p, :, cols] = gq[i * half : (i + 1) * half]
                here = slice(i * part, (i + 1) * part)
                gkv_s[i, :, p, :, cols] = gk[here].reshape(layers, rows, 2 * HD)
                gkv_s[i, :, p, :, more] = gv[here].reshape(layers, rows, 2 * HD)
    gq_all = gq_s[...].reshape(2 * prompts * half, width)
    gkv_all = gkv_s[...].reshape(2 * prompts * part, 2 * width)
    block = 256
    for begin in range(0, channels, block):
        at = pl.ds(begin, block)
        x = both([t[:, :, at].reshape(prompts * half, block) for t in tokens])
        n = both([t[:, :, :, at].reshape(prompts * part, block) for t in maps])
        dq = lax.dot_general(x, gq_all, TN, preferred_element_type=F32)
        dkv = lax.dot_general(n, gkv_all, TN, preferred_element_type=F32)
        for i, total in enumerate((dq, dkv[:, :width], dkv[:, width:])):
            if before is None:
                sums[i, at] = total
            else:
                total = (total + before[i, at]).astype(BF16)
                share = sums.shape[2]
                own = begin // share
                sums[own : own + block // share, i] = total.reshape(
                    block // share, share, width
                )


def attention(core, xo, xt, uo, ut, no, nt, weights, before, chunk, owners):
    layers, prompts, rows, channels = no.shape
    half = xo.shape[1]
    part = layers * rows
    local = weights.shape[1] // 3
    step = min(local, 4 * HD)
    steps = local // step
    token_spec = pl.BlockSpec((prompts, half, channels), lambda c, core: (chunk, 0, 0))
    up_spec = pl.BlockSpec((prompts, half, step), lambda c, core: (chunk, 0, c + core[0] * steps))
    map_spec = whole(pltpu.VMEM)
    w_specs = [
        pl.BlockSpec((channels, step), lambda c, core, i=i: (0, c + i * steps)) for i in range(3)
    ]
    grad_spec = pl.BlockSpec((prompts, half, step), lambda c, core: (0, 0, c))
    wide_spec = pl.BlockSpec((3, channels, step), lambda c, core: (0, 0, c))
    has_before = before is not None
    if has_before:
        share = channels // owners
        sum_shape = jax.ShapeDtypeStruct((owners, 3, share, local), BF16)
        sum_spec = pl.BlockSpec((owners, 3, share, step), lambda c, core: (0, 0, 0, c))
    else:
        sum_shape = jax.ShapeDtypeStruct((3, channels, local), F32)
        sum_spec = wide_spec
    return pl.pallas_call(
        functools.partial(attention_kernel, has_before),
        out_shape=[jax.ShapeDtypeStruct((prompts, half, local), BF16)] * 2 + [sum_shape],
        grid_spec=pltpu.PrefetchScalarGridSpec(
            num_scalar_prefetch=1,
            grid=(steps,),
            in_specs=[token_spec, token_spec, up_spec, up_spec, map_spec, map_spec]
            + w_specs
            + [wide_spec] * has_before,
            out_specs=[grad_spec, grad_spec, sum_spec],
            scratch_shapes=[
                pltpu.VMEM((2, prompts, half, step), BF16),
                pltpu.VMEM((2, layers, prompts, rows, step), BF16),
                pltpu.VMEM((2, layers, prompts, rows, step), BF16),
                pltpu.VMEM((2, prompts, half, step), BF16),
                pltpu.VMEM((2, layers, prompts, rows, 2 * step), BF16),
            ],
        ),
        compiler_params=pltpu.CompilerParams(vmem_limit_bytes=50 * 2**20),
        cost_estimate=pl.CostEstimate(
            flops=prompts * 2 * 2 * (2 * half + 4 * part) * channels * local,
            bytes_accessed=16 * 2**20,
            transcendentals=prompts * 2 * half * 2 * part * (local // HD),
        ),
        name="attention",
    )(core, xo, xt, uo, ut, no, nt, weights, weights, weights, *([before] if has_before else []))


def hold(array, after):
    anywhere = pl.BlockSpec(memory_space=pl.ANY)
    return pl.pallas_call(
        lambda array_ref, after_ref, out_ref: None,
        out_shape=jax.ShapeDtypeStruct(array.shape, array.dtype),
        in_specs=[anywhere, anywhere],
        out_specs=anywhere,
        input_output_aliases={0: 0},
        name="hold",
    )(array, after)


def per_device(
    features,
    store_maps,
    neighbour_owner,
    neighbour_slot,
    query_weight,
    key_weight,
    value_weight,
    grad_context,
):
    prompts, half, channels = features.shape
    entries = store_maps.shape[0]
    owners = lax.axis_size("store")
    layers = lax.axis_size("batch")
    local = query_weight.shape[1]
    layer, core = lax.axis_index("batch"), lax.axis_index("space")
    swap = [(0, 1), (1, 0)]

    share = half // layers
    spread, packed = prepare(
        layer, store_maps, query_weight, key_weight, value_weight, owners, share
    )
    table = lax.all_to_all(
        spread, "store", split_axis=0, concat_axis=0, tiled=True
    ).reshape(owners * entries, share, channels)

    listed = (neighbour_owner * entries + neighbour_slot).reshape(1, -1)
    reach = 1
    while reach < layers:
        moved = lax.ppermute(
            listed, "batch", [(z, (z + reach) % layers) for z in range(layers)]
        )
        listed = jnp.concatenate([listed, moved], axis=0)
        reach *= 2
    place = jnp.roll(listed[::-1], layer + 1, axis=0)
    chunks = 2
    per_chunk = prompts // chunks
    per = 2 * per_chunk
    order = place.reshape(layers, chunks, per).transpose(1, 0, 2).reshape(-1)
    x_other = lax.ppermute(features, "space", swap)
    u_other = lax.ppermute(grad_context, "space", swap)
    picked = pick(table, order, chunks, layers, per, [x_other, u_other])

    weights = lax.all_gather(packed, "store", axis=0, tiled=True)
    full_query = weights[:, :local]

    sums = gq = None
    features_out = []
    for chunk in range(chunks):
        n_own = lax.all_to_all(
            picked[chunk], "batch", split_axis=0, concat_axis=0, tiled=True
        ).reshape(layers, per_chunk, 2 * share, channels)
        if gq is not None:
            n_own = hold(n_own, gq)
        n_other = lax.ppermute(n_own, "space", swap)
        gq, gq_other, sums = attention(
            core.reshape(1).astype(jnp.int32),
            features, x_other, grad_context, u_other, n_own, n_other,
            weights, sums, chunk, owners,
        )

        def rows_of(grad):
            product = lax.dot_general(
                grad, full_query, (((2,), (1,)), ((), ())), preferred_element_type=F32
            )
            return lax.reduce_precision(product, exponent_bits=8, mantissa_bits=7)

        received = lax.ppermute(rows_of(gq_other).astype(BF16), "space", swap)
        features_out.append((rows_of(gq) + received.astype(F32)).astype(BF16))
    grad_features = jnp.concatenate(features_out, axis=0)

    row_share = channels // owners
    came = lax.all_to_all(sums, "store", split_axis=0, concat_axis=0, tiled=True)
    layer_sum = jnp.sum(came.astype(F32), axis=0)
    share = row_share // layers
    pieces = layer_sum.reshape(3, layers, share, local).transpose(1, 0, 2, 3)
    crossed = lax.all_to_all(pieces, "batch", split_axis=0, concat_axis=0, tiled=True)
    totals = lax.all_to_all(
        total_for_all(crossed), "batch", split_axis=0, concat_axis=0, tiled=True
    )
    grads = [totals[:, i].reshape(row_share, local) for i in range(3)]
    return (grad_features, *grads)


def solution(mesh):
    in_specs = (
        P(("store", "batch"), "space", None),
        P("store", "space", None),
        P(("store", "batch"), None),
        P(("store", "batch"), None),
        P("store", "space"),
        P("store", "space"),
        P("store", "space"),
        P(("store", "batch"), "space", None),
    )
    out_specs = (
        P(("store", "batch"), "space", None),
        P("store", "space"),
        P("store", "space"),
        P("store", "space"),
    )
    return jax.shard_map(
        per_device, mesh=mesh, in_specs=in_specs, out_specs=out_specs, check_vma=False
    )
```

```python
import functools

import jax
import jax.numpy as jnp
from jax import lax
from jax.experimental import pallas as pl
from jax.experimental.pallas import tpu as pltpu
from jax.sharding import PartitionSpec as P

HD = 64
VMEM_BYTES = 60 * 2**20
F32 = jnp.float32
BF16 = jnp.bfloat16
NT = (((1,), (1,)), ((), ()))
TN = (((0,), (0,)), ((), ()))


def whole(memory):
    return pl.BlockSpec(memory_space=memory)


def prepare_kernel(layer_ref, maps_ref, wq, wk, wv, table_ref, packed_ref):
    owners, _, share, _ = table_ref.shape
    begin = pl.multiple_of(layer_ref[0] * share, share)
    mine = maps_ref[:, pl.ds(begin, share), :]
    for owner in range(owners):
        table_ref[owner] = mine
    local = wq.shape[1]
    for i, w in enumerate((wq, wk, wv)):
        packed_ref[:, pl.ds(i * local, local)] = w[...]


def prepare(layer, store_maps, wq, wk, wv, owners, share):
    entries, _, channels = store_maps.shape
    rows, local = wq.shape
    vmem = pl.BlockSpec(memory_space=pltpu.VMEM)
    return pl.pallas_call(
        prepare_kernel,
        out_shape=[
            jax.ShapeDtypeStruct((owners, entries, share, channels), BF16),
            jax.ShapeDtypeStruct((rows, 3 * local), BF16),
        ],
        in_specs=[pl.BlockSpec(memory_space=pltpu.SMEM)] + [vmem] * 4,
        out_specs=[vmem] * 2,
        compiler_params=pltpu.CompilerParams(vmem_limit_bytes=VMEM_BYTES),
        name="prepare",
    )(layer.reshape(1).astype(jnp.int32), store_maps, wq, wk, wv)


def total_kernel(parts_ref, out_ref):
    total = parts_ref[0]
    for i in range(1, parts_ref.shape[0]):
        total = total + parts_ref[i]
    for i in range(out_ref.shape[0]):
        out_ref[i] = total


def total_for_all(parts):
    return pl.pallas_call(
        total_kernel,
        out_shape=jax.ShapeDtypeStruct(parts.shape, parts.dtype),
        in_specs=[whole(pltpu.VMEM)],
        out_specs=whole(pltpu.VMEM),
        compiler_params=pltpu.CompilerParams(vmem_limit_bytes=16 * 2**20),
        name="total",
    )(parts)


def pick_kernel(waits, where_ref, table_ref, *refs):
    outs = refs[waits:]
    layers, per = outs[0].shape[:2]
    for number, out in enumerate(outs):
        for layer in range(layers):
            for item in range(per):
                place = where_ref[(number * layers + layer) * per + item]
                out[layer, item] = table_ref[place]


def pick(table, where, chunks, layers, per, after):
    rows, channels = table.shape[1:]
    vmem = pl.BlockSpec(memory_space=pltpu.VMEM)
    return pl.pallas_call(
        functools.partial(pick_kernel, len(after)),
        out_shape=[jax.ShapeDtypeStruct((layers, per, rows, channels), table.dtype)] * chunks,
        in_specs=[whole(pltpu.SMEM), vmem] + [whole(pl.ANY)] * len(after),
        out_specs=[vmem] * chunks,
        compiler_params=pltpu.CompilerParams(vmem_limit_bytes=16 * 2**20),
        name="pick",
    )(where, table, *after)


def attention_kernel(has_before, core_ref, *refs):
    xo, xt, uo, ut, no, nt, wq, wk, wv = refs[:9]
    before = refs[9] if has_before else None
    gqo, gqt, sums, q_s, k_s, v_s, gq_s, gkv_s = refs[9 + has_before :]
    prompts, half, channels = xo.shape
    layers, _, rows, _ = no.shape
    part = layers * rows
    width = wq.shape[1]
    tokens, maps = (xo, xt), (no, nt)
    for i in range(2):
        x = tokens[i][...].reshape(prompts * half, channels)
        n = maps[i][...].reshape(prompts * part, channels)
        q = jnp.dot(x, wq[...], preferred_element_type=F32).astype(BF16)
        k = jnp.dot(n, wk[...], preferred_element_type=F32).astype(BF16)
        v = jnp.dot(n, wv[...], preferred_element_type=F32).astype(BF16)
        q_s[i] = q.reshape(prompts, half, width)
        k_s[i] = k.reshape(layers, prompts, rows, width)
        v_s[i] = v.reshape(layers, prompts, rows, width)
    scale = HD ** (-0.5)
    lane = lax.broadcasted_iota(jnp.int32, (1, 2 * HD), 1)
    keeps = [jnp.where(lane < HD, 1.0, 0.0), jnp.where(lane < HD, 0.0, 1.0)]

    def both(array):
        return jnp.concatenate([array[0], array[1]], axis=0)

    def start(p, pair):
        cols = pl.ds(pair * 2 * HD, 2 * HD)
        kp = both([k_s[i, :, p, :, cols].reshape(part, 2 * HD) for i in range(2)])
        vp = both([v_s[i, :, p, :, cols].reshape(part, 2 * HD) for i in range(2)])
        qp = both([q_s[i, p, :, cols] for i in range(2)])
        up = both([uo[p, :, cols], ut[p, :, cols]])
        qm = [qp * (k * scale).astype(BF16) for k in keeps]
        um = [up * k.astype(BF16) for k in keeps]
        s = [lax.dot_general(kp, q, NT, preferred_element_type=F32) for q in qm]
        dw = [lax.dot_general(vp, u, NT, preferred_element_type=F32) for u in um]
        return kp, qm, um, s, dw

    def finish(p, pair, kp, qm, um, s, dw):
        cols = pl.ds(pair * 2 * HD, 2 * HD)
        kt = kp.T
        grad_k = grad_v = None
        grad_q = []
        for side in range(2):
            e = jnp.exp(s[side] - jnp.max(s[side], axis=0, keepdims=True))
            inverse = 1.0 / jnp.sum(e, axis=0, keepdims=True)
            att = e * inverse
            row = jnp.sum(e * dw[side], axis=0, keepdims=True) * inverse
            gv_part = jnp.dot(att.astype(BF16), um[side], preferred_element_type=F32)
            ds = (att * (dw[side] - row)).astype(BF16)
            gk_part = jnp.dot(ds, qm[side], preferred_element_type=F32)
            grad_q.append(
                jnp.dot(kt[side * HD : (side + 1) * HD], ds, preferred_element_type=F32)
            )
            grad_v = gv_part if grad_v is None else grad_v + gv_part
            grad_k = gk_part if grad_k is None else grad_k + gk_part
        gq = (both(grad_q) * scale).T.astype(BF16)
        gk, gv = grad_k.astype(BF16), grad_v.astype(BF16)
        more = pl.ds(width + pair * 2 * HD, 2 * HD)
        for i, out in enumerate((gqo, gqt)):
            out[p, :, cols] = gq[i * half : (i + 1) * half]
            gq_s[i, p, :, cols] = gq[i * half : (i + 1) * half]
            here = slice(i * part, (i + 1) * part)
            gkv_s[i, :, p, :, cols] = gk[here].reshape(layers, rows, 2 * HD)
            gkv_s[i, :, p, :, more] = gv[here].reshape(layers, rows, 2 * HD)

    units = [(p, pair) for p in range(prompts) for pair in range(width // (2 * HD))]
    held = start(*units[0])
    for i, unit in enumerate(units):
        later = start(*units[i + 1]) if i + 1 < len(units) else None
        finish(*unit, *held)
        held = later
    gq_all = gq_s[...].reshape(2 * prompts * half, width)
    gkv_all = gkv_s[...].reshape(2 * prompts * part, 2 * width)
    block = 256
    for begin in range(0, channels, block):
        at = pl.ds(begin, block)
        x = both([t[:, :, at].reshape(prompts * half, block) for t in tokens])
        n = both([t[:, :, :, at].reshape(prompts * part, block) for t in maps])
        dq = lax.dot_general(x, gq_all, TN, preferred_element_type=F32)
        dkv = lax.dot_general(n, gkv_all, TN, preferred_element_type=F32)
        for i, total in enumerate((dq, dkv[:, :width], dkv[:, width:])):
            if before is None:
                sums[i, at] = total
            else:
                total = (total + before[i, at]).astype(BF16)
                share = sums.shape[2]
                own = begin // share
                sums[own : own + block // share, i] = total.reshape(
                    block // share, share, width
                )


def attention(core, xo, xt, uo, ut, no, nt, weights, before, chunk, owners):
    layers, prompts, rows, channels = no.shape
    half = xo.shape[1]
    part = layers * rows
    local = weights.shape[1] // 3
    step = min(local, 4 * HD)
    steps = local // step
    token_spec = pl.BlockSpec((prompts, half, channels), lambda c, core: (chunk, 0, 0))
    up_spec = pl.BlockSpec((prompts, half, step), lambda c, core: (chunk, 0, c + core[0] * steps))
    map_spec = whole(pltpu.VMEM)
    w_specs = [
        pl.BlockSpec((channels, step), lambda c, core, i=i: (0, c + i * steps)) for i in range(3)
    ]
    grad_spec = pl.BlockSpec((prompts, half, step), lambda c, core: (0, 0, c))
    wide_spec = pl.BlockSpec((3, channels, step), lambda c, core: (0, 0, c))
    has_before = before is not None
    if has_before:
        share = channels // owners
        sum_shape = jax.ShapeDtypeStruct((owners, 3, share, local), BF16)
        sum_spec = pl.BlockSpec((owners, 3, share, step), lambda c, core: (0, 0, 0, c))
    else:
        sum_shape = jax.ShapeDtypeStruct((3, channels, local), F32)
        sum_spec = wide_spec
    return pl.pallas_call(
        functools.partial(attention_kernel, has_before),
        out_shape=[jax.ShapeDtypeStruct((prompts, half, local), BF16)] * 2 + [sum_shape],
        grid_spec=pltpu.PrefetchScalarGridSpec(
            num_scalar_prefetch=1,
            grid=(steps,),
            in_specs=[token_spec, token_spec, up_spec, up_spec, map_spec, map_spec]
            + w_specs
            + [wide_spec] * has_before,
            out_specs=[grad_spec, grad_spec, sum_spec],
            scratch_shapes=[
                pltpu.VMEM((2, prompts, half, step), BF16),
                pltpu.VMEM((2, layers, prompts, rows, step), BF16),
                pltpu.VMEM((2, layers, prompts, rows, step), BF16),
                pltpu.VMEM((2, prompts, half, step), BF16),
                pltpu.VMEM((2, layers, prompts, rows, 2 * step), BF16),
            ],
        ),
        compiler_params=pltpu.CompilerParams(vmem_limit_bytes=50 * 2**20),
        cost_estimate=pl.CostEstimate(
            flops=prompts * 2 * 2 * (2 * half + 4 * part) * channels * local,
            bytes_accessed=16 * 2**20,
            transcendentals=prompts * 2 * half * 2 * part * (local // HD),
        ),
        name="attention",
    )(core, xo, xt, uo, ut, no, nt, weights, weights, weights, *([before] if has_before else []))


def hold(array, after):
    anywhere = pl.BlockSpec(memory_space=pl.ANY)
    return pl.pallas_call(
        lambda array_ref, after_ref, out_ref: None,
        out_shape=jax.ShapeDtypeStruct(array.shape, array.dtype),
        in_specs=[anywhere, anywhere],
        out_specs=anywhere,
        input_output_aliases={0: 0},
        name="hold",
    )(array, after)


def per_device(
    features,
    store_maps,
    neighbour_owner,
    neighbour_slot,
    query_weight,
    key_weight,
    value_weight,
    grad_context,
):
    prompts, half, channels = features.shape
    entries = store_maps.shape[0]
    owners = lax.axis_size("store")
    layers = lax.axis_size("batch")
    local = query_weight.shape[1]
    layer, core = lax.axis_index("batch"), lax.axis_index("space")
    swap = [(0, 1), (1, 0)]

    share = half // layers
    spread, packed = prepare(
        layer, store_maps, query_weight, key_weight, value_weight, owners, share
    )
    table = lax.all_to_all(
        spread, "store", split_axis=0, concat_axis=0, tiled=True
    ).reshape(owners * entries, share, channels)

    listed = (neighbour_owner * entries + neighbour_slot).reshape(1, -1)
    reach = 1
    while reach < layers:
        moved = lax.ppermute(
            listed, "batch", [(z, (z + reach) % layers) for z in range(layers)]
        )
        listed = jnp.concatenate([listed, moved], axis=0)
        reach *= 2
    place = jnp.roll(listed[::-1], layer + 1, axis=0)
    chunks = 2
    per_chunk = prompts // chunks
    per = 2 * per_chunk
    order = place.reshape(layers, chunks, per).transpose(1, 0, 2).reshape(-1)
    x_other = lax.ppermute(features, "space", swap)
    u_other = lax.ppermute(grad_context, "space", swap)
    picked = pick(table, order, chunks, layers, per, [x_other, u_other])

    weights = lax.all_gather(packed, "store", axis=0, tiled=True)
    full_query = weights[:, :local]

    sums = gq = None
    features_out = []
    for chunk in range(chunks):
        n_own = lax.all_to_all(
            picked[chunk], "batch", split_axis=0, concat_axis=0, tiled=True
        ).reshape(layers, per_chunk, 2 * share, channels)
        if gq is not None:
            n_own = hold(n_own, gq)
        n_other = lax.ppermute(n_own, "space", swap)
        gq, gq_other, sums = attention(
            core.reshape(1).astype(jnp.int32),
            features, x_other, grad_context, u_other, n_own, n_other,
            weights, sums, chunk, owners,
        )

        def rows_of(grad):
            product = lax.dot_general(
                grad, full_query, (((2,), (1,)), ((), ())), preferred_element_type=F32
            )
            return lax.reduce_precision(product, exponent_bits=8, mantissa_bits=7)

        received = lax.ppermute(rows_of(gq_other).astype(BF16), "space", swap)
        features_out.append((rows_of(gq) + received.astype(F32)).astype(BF16))
    grad_features = jnp.concatenate(features_out, axis=0)

    row_share = channels // owners
    came = lax.all_to_all(sums, "store", split_axis=0, concat_axis=0, tiled=True)
    layer_sum = jnp.sum(came.astype(F32), axis=0)
    share = row_share // layers
    pieces = layer_sum.reshape(3, layers, share, local).transpose(1, 0, 2, 3)
    crossed = lax.all_to_all(pieces, "batch", split_axis=0, concat_axis=0, tiled=True)
    totals = lax.all_to_all(
        total_for_all(crossed), "batch", split_axis=0, concat_axis=0, tiled=True
    )
    grads = [totals[:, i].reshape(row_share, local) for i in range(3)]
    return (grad_features, *grads)


def solution(mesh):
    in_specs = (
        P(("store", "batch"), "space", None),
        P("store", "space", None),
        P(("store", "batch"), None),
        P(("store", "batch"), None),
        P("store", "space"),
        P("store", "space"),
        P("store", "space"),
        P(("store", "batch"), "space", None),
    )
    out_specs = (
        P(("store", "batch"), "space", None),
        P("store", "space"),
        P("store", "space"),
        P("store", "space"),
    )
    return jax.shard_map(
        per_device, mesh=mesh, in_specs=in_specs, out_specs=out_specs, check_vma=False
    )
```

```python
import functools

import jax
import jax.numpy as jnp
from jax import lax
from jax.experimental import pallas as pl
from jax.experimental.pallas import tpu as pltpu
from jax.sharding import PartitionSpec as P

HD = 64
VMEM_BYTES = 60 * 2**20
F32 = jnp.float32
BF16 = jnp.bfloat16
NT = (((1,), (1,)), ((), ()))
TN = (((0,), (0,)), ((), ()))


def whole(memory):
    return pl.BlockSpec(memory_space=memory)


def prepare_kernel(layer_ref, maps_ref, wq, wk, wv, table_ref, packed_ref):
    owners, _, share, _ = table_ref.shape
    begin = pl.multiple_of(layer_ref[0] * share, share)
    mine = maps_ref[:, pl.ds(begin, share), :]
    for owner in range(owners):
        table_ref[owner] = mine
    local = wq.shape[1]
    for i, w in enumerate((wq, wk, wv)):
        packed_ref[:, pl.ds(i * local, local)] = w[...]


def prepare(layer, store_maps, wq, wk, wv, owners, share):
    entries, _, channels = store_maps.shape
    rows, local = wq.shape
    vmem = pl.BlockSpec(memory_space=pltpu.VMEM)
    return pl.pallas_call(
        prepare_kernel,
        out_shape=[
            jax.ShapeDtypeStruct((owners, entries, share, channels), BF16),
            jax.ShapeDtypeStruct((rows, 3 * local), BF16),
        ],
        in_specs=[pl.BlockSpec(memory_space=pltpu.SMEM)] + [vmem] * 4,
        out_specs=[vmem] * 2,
        compiler_params=pltpu.CompilerParams(vmem_limit_bytes=VMEM_BYTES),
        name="prepare",
    )(layer.reshape(1).astype(jnp.int32), store_maps, wq, wk, wv)


def total_kernel(parts_ref, out_ref):
    total = parts_ref[0]
    for i in range(1, parts_ref.shape[0]):
        total = total + parts_ref[i]
    for i in range(out_ref.shape[0]):
        out_ref[i] = total


def total_for_all(parts):
    return pl.pallas_call(
        total_kernel,
        out_shape=jax.ShapeDtypeStruct(parts.shape, parts.dtype),
        in_specs=[whole(pltpu.VMEM)],
        out_specs=whole(pltpu.VMEM),
        compiler_params=pltpu.CompilerParams(vmem_limit_bytes=16 * 2**20),
        name="total",
    )(parts)


def pick_kernel(waits, where_ref, table_ref, *refs):
    outs = refs[waits:]
    layers, per = outs[0].shape[:2]
    for number, out in enumerate(outs):
        for layer in range(layers):
            for item in range(per):
                place = where_ref[(number * layers + layer) * per + item]
                out[layer, item] = table_ref[place]


def pick(table, where, chunks, layers, per, after):
    rows, channels = table.shape[1:]
    vmem = pl.BlockSpec(memory_space=pltpu.VMEM)
    return pl.pallas_call(
        functools.partial(pick_kernel, len(after)),
        out_shape=[jax.ShapeDtypeStruct((layers, per, rows, channels), table.dtype)] * chunks,
        in_specs=[whole(pltpu.SMEM), vmem] + [whole(pl.ANY)] * len(after),
        out_specs=[vmem] * chunks,
        compiler_params=pltpu.CompilerParams(vmem_limit_bytes=16 * 2**20),
        name="pick",
    )(where, table, *after)


def attention_kernel(has_before, core_ref, *refs):
    xo, xt, uo, ut, no, nt, wq, wk, wv = refs[:9]
    before = refs[9] if has_before else None
    gqo, gqt, sums, q_s, k_s, v_s, gq_s, gkv_s, *early = refs[9 + has_before :]
    prompts, half, channels = xo.shape
    layers, _, rows, _ = no.shape
    part = layers * rows
    width = wq.shape[1]
    if has_before:
        before_s, arrived = early
        at_step = pl.multiple_of(pl.program_id(0) * width, width)
        fetch = pltpu.make_async_copy(before.at[:, :, pl.ds(at_step, width)], before_s, arrived)
        fetch.start()
    tokens, maps = (xo, xt), (no, nt)
    for i in range(2):
        x = tokens[i][...].reshape(prompts * half, channels)
        n = maps[i][...].reshape(prompts * part, channels)
        q = jnp.dot(x, wq[...], preferred_element_type=F32).astype(BF16)
        k = jnp.dot(n, wk[...], preferred_element_type=F32).astype(BF16)
        v = jnp.dot(n, wv[...], preferred_element_type=F32).astype(BF16)
        q_s[i] = q.reshape(prompts, half, width)
        k_s[i] = k.reshape(layers, prompts, rows, width)
        v_s[i] = v.reshape(layers, prompts, rows, width)
    scale = HD ** (-0.5)
    lane = lax.broadcasted_iota(jnp.int32, (1, 2 * HD), 1)
    keeps = [jnp.where(lane < HD, 1.0, 0.0), jnp.where(lane < HD, 0.0, 1.0)]

    def both(array):
        return jnp.concatenate([array[0], array[1]], axis=0)

    def start(p, pair):
        cols = pl.ds(pair * 2 * HD, 2 * HD)
        kp = both([k_s[i, :, p, :, cols].reshape(part, 2 * HD) for i in range(2)])
        vp = both([v_s[i, :, p, :, cols].reshape(part, 2 * HD) for i in range(2)])
        qp = both([q_s[i, p, :, cols] for i in range(2)])
        up = both([uo[p, :, cols], ut[p, :, cols]])
        qm = [qp * (k * scale).astype(BF16) for k in keeps]
        um = [up * k.astype(BF16) for k in keeps]
        s = [lax.dot_general(kp, q, NT, preferred_element_type=F32) for q in qm]
        dw = [lax.dot_general(vp, u, NT, preferred_element_type=F32) for u in um]
        return kp, qm, um, s, dw

    def finish(p, pair, kp, qm, um, s, dw):
        cols = pl.ds(pair * 2 * HD, 2 * HD)
        kt = kp.T
        grad_k = grad_v = None
        grad_q = []
        for side in range(2):
            e = jnp.exp(s[side] - jnp.max(s[side], axis=0, keepdims=True))
            inverse = 1.0 / jnp.sum(e, axis=0, keepdims=True)
            att = e * inverse
            row = jnp.sum(e * dw[side], axis=0, keepdims=True) * inverse
            gv_part = jnp.dot(att.astype(BF16), um[side], preferred_element_type=F32)
            ds = (att * (dw[side] - row)).astype(BF16)
            gk_part = jnp.dot(ds, qm[side], preferred_element_type=F32)
            grad_q.append(
                jnp.dot(kt[side * HD : (side + 1) * HD], ds, preferred_element_type=F32)
            )
            grad_v = gv_part if grad_v is None else grad_v + gv_part
            grad_k = gk_part if grad_k is None else grad_k + gk_part
        gq = (both(grad_q) * scale).T.astype(BF16)
        gk, gv = grad_k.astype(BF16), grad_v.astype(BF16)
        more = pl.ds(width + pair * 2 * HD, 2 * HD)
        for i, out in enumerate((gqo, gqt)):
            out[p, :, cols] = gq[i * half : (i + 1) * half]
            gq_s[i, p, :, cols] = gq[i * half : (i + 1) * half]
            here = slice(i * part, (i + 1) * part)
            gkv_s[i, :, p, :, cols] = gk[here].reshape(layers, rows, 2 * HD)
            gkv_s[i, :, p, :, more] = gv[here].reshape(layers, rows, 2 * HD)

    units = [(p, pair) for p in range(prompts) for pair in range(width // (2 * HD))]
    held = start(*units[0])
    for i, unit in enumerate(units):
        later = start(*units[i + 1]) if i + 1 < len(units) else None
        finish(*unit, *held)
        held = later
    if has_before:
        fetch.wait()
    gq_all = gq_s[...].reshape(2 * prompts * half, width)
    gkv_all = gkv_s[...].reshape(2 * prompts * part, 2 * width)
    block = 256
    for begin in range(0, channels, block):
        at = pl.ds(begin, block)
        x = both([t[:, :, at].reshape(prompts * half, block) for t in tokens])
        n = both([t[:, :, :, at].reshape(prompts * part, block) for t in maps])
        dq = lax.dot_general(x, gq_all, TN, preferred_element_type=F32)
        dkv = lax.dot_general(n, gkv_all, TN, preferred_element_type=F32)
        for i, total in enumerate((dq, dkv[:, :width], dkv[:, width:])):
            if before is None:
                sums[i, at] = total
            else:
                total = (total + before_s[i, at]).astype(BF16)
                share = sums.shape[2]
                own = begin // share
                sums[own : own + block // share, i] = total.reshape(
                    block // share, share, width
                )


def attention(core, xo, xt, uo, ut, no, nt, weights, before, chunk, owners):
    layers, prompts, rows, channels = no.shape
    half = xo.shape[1]
    part = layers * rows
    local = weights.shape[1] // 3
    step = min(local, 4 * HD)
    steps = local // step
    token_spec = pl.BlockSpec((prompts, half, channels), lambda c, core: (chunk, 0, 0))
    up_spec = pl.BlockSpec((prompts, half, step), lambda c, core: (chunk, 0, c + core[0] * steps))
    map_spec = whole(pltpu.VMEM)
    w_specs = [
        pl.BlockSpec((channels, step), lambda c, core, i=i: (0, c + i * steps)) for i in range(3)
    ]
    grad_spec = pl.BlockSpec((prompts, half, step), lambda c, core: (0, 0, c))
    wide_spec = pl.BlockSpec((3, channels, step), lambda c, core: (0, 0, c))
    has_before = before is not None
    if has_before:
        share = channels // owners
        sum_shape = jax.ShapeDtypeStruct((owners, 3, share, local), BF16)
        sum_spec = pl.BlockSpec((owners, 3, share, step), lambda c, core: (0, 0, 0, c))
    else:
        sum_shape = jax.ShapeDtypeStruct((3, channels, local), F32)
        sum_spec = wide_spec
    return pl.pallas_call(
        functools.partial(attention_kernel, has_before),
        out_shape=[jax.ShapeDtypeStruct((prompts, half, local), BF16)] * 2 + [sum_shape],
        grid_spec=pltpu.PrefetchScalarGridSpec(
            num_scalar_prefetch=1,
            grid=(steps,),
            in_specs=[token_spec, token_spec, up_spec, up_spec, map_spec, map_spec]
            + w_specs
            + [whole(pl.ANY)] * has_before,
            out_specs=[grad_spec, grad_spec, sum_spec],
            scratch_shapes=[
                pltpu.VMEM((2, prompts, half, step), BF16),
                pltpu.VMEM((2, layers, prompts, rows, step), BF16),
                pltpu.VMEM((2, layers, prompts, rows, step), BF16),
                pltpu.VMEM((2, prompts, half, step), BF16),
                pltpu.VMEM((2, layers, prompts, rows, 2 * step), BF16),
            ]
            + [pltpu.VMEM((3, channels, step), F32), pltpu.SemaphoreType.DMA] * has_before,
        ),
        compiler_params=pltpu.CompilerParams(vmem_limit_bytes=50 * 2**20),
        cost_estimate=pl.CostEstimate(
            flops=prompts * 2 * 2 * (2 * half + 4 * part) * channels * local,
            bytes_accessed=16 * 2**20,
            transcendentals=prompts * 2 * half * 2 * part * (local // HD),
        ),
        name="attention",
    )(core, xo, xt, uo, ut, no, nt, weights, weights, weights, *([before] if has_before else []))


def hold(array, after):
    anywhere = pl.BlockSpec(memory_space=pl.ANY)
    return pl.pallas_call(
        lambda array_ref, after_ref, out_ref: None,
        out_shape=jax.ShapeDtypeStruct(array.shape, array.dtype),
        in_specs=[anywhere, anywhere],
        out_specs=anywhere,
        input_output_aliases={0: 0},
        name="hold",
    )(array, after)


def per_device(
    features,
    store_maps,
    neighbour_owner,
    neighbour_slot,
    query_weight,
    key_weight,
    value_weight,
    grad_context,
):
    prompts, half, channels = features.shape
    entries = store_maps.shape[0]
    owners = lax.axis_size("store")
    layers = lax.axis_size("batch")
    local = query_weight.shape[1]
    layer, core = lax.axis_index("batch"), lax.axis_index("space")
    swap = [(0, 1), (1, 0)]

    share = half // layers
    spread, packed = prepare(
        layer, store_maps, query_weight, key_weight, value_weight, owners, share
    )
    table = lax.all_to_all(
        spread, "store", split_axis=0, concat_axis=0, tiled=True
    ).reshape(owners * entries, share, channels)

    listed = (neighbour_owner * entries + neighbour_slot).reshape(1, -1)
    reach = 1
    while reach < layers:
        moved = lax.ppermute(
            listed, "batch", [(z, (z + reach) % layers) for z in range(layers)]
        )
        listed = jnp.concatenate([listed, moved], axis=0)
        reach *= 2
    place = jnp.roll(listed[::-1], layer + 1, axis=0)
    chunks = 2
    per_chunk = prompts // chunks
    per = 2 * per_chunk
    order = place.reshape(layers, chunks, per).transpose(1, 0, 2).reshape(-1)
    x_other = lax.ppermute(features, "space", swap)
    u_other = lax.ppermute(grad_context, "space", swap)
    picked = pick(table, order, chunks, layers, per, [x_other, u_other])

    weights = lax.all_gather(packed, "store", axis=0, tiled=True)
    full_query = weights[:, :local]

    sums = gq = None
    features_out = []
    for chunk in range(chunks):
        n_own = lax.all_to_all(
            picked[chunk], "batch", split_axis=0, concat_axis=0, tiled=True
        ).reshape(layers, per_chunk, 2 * share, channels)
        if gq is not None:
            n_own = hold(n_own, gq)
        n_other = lax.ppermute(n_own, "space", swap)
        gq, gq_other, sums = attention(
            core.reshape(1).astype(jnp.int32),
            features, x_other, grad_context, u_other, n_own, n_other,
            weights, sums, chunk, owners,
        )

        def rows_of(grad):
            product = lax.dot_general(
                grad, full_query, (((2,), (1,)), ((), ())), preferred_element_type=F32
            )
            return lax.reduce_precision(product, exponent_bits=8, mantissa_bits=7)

        received = lax.ppermute(rows_of(gq_other).astype(BF16), "space", swap)
        features_out.append((rows_of(gq) + received.astype(F32)).astype(BF16))
    grad_features = jnp.concatenate(features_out, axis=0)

    row_share = channels // owners
    came = lax.all_to_all(sums, "store", split_axis=0, concat_axis=0, tiled=True)
    layer_sum = jnp.sum(came.astype(F32), axis=0)
    share = row_share // layers
    pieces = layer_sum.reshape(3, layers, share, local).transpose(1, 0, 2, 3)
    crossed = lax.all_to_all(pieces, "batch", split_axis=0, concat_axis=0, tiled=True)
    totals = lax.all_to_all(
        total_for_all(crossed), "batch", split_axis=0, concat_axis=0, tiled=True
    )
    grads = [totals[:, i].reshape(row_share, local) for i in range(3)]
    return (grad_features, *grads)


def solution(mesh):
    in_specs = (
        P(("store", "batch"), "space", None),
        P("store", "space", None),
        P(("store", "batch"), None),
        P(("store", "batch"), None),
        P("store", "space"),
        P("store", "space"),
        P("store", "space"),
        P(("store", "batch"), "space", None),
    )
    out_specs = (
        P(("store", "batch"), "space", None),
        P("store", "space"),
        P("store", "space"),
        P("store", "space"),
    )
    return jax.shard_map(
        per_device, mesh=mesh, in_specs=in_specs, out_specs=out_specs, check_vma=False
    )
```
